512 devices in a mesh: row: 32 (over x, y, core), col: 16 (over z).
Axes of the slice: x: 4, y: 4, z: 16, core: 2. Of those that a mesh axis runs over, the one named last changes fastest.
Arguments:
- transition: bfloat16 [8192, 8192], P('row', 'col'), may hold values from 0.0099487305 to 1
- tile_live: int32 [64, 64], replicated, may hold values from 0 to 1, as said below
- prune_keep: int32 [8192, 8192], P('row', 'col'), may hold values from 0 to 1, as said below
Outputs:
- next_strips: float32 [16, 512, 8192], P('col', 'row')
The draws below stay inside these ranges and needn't reach their ends.
Inputs may be any that keep to these rules, and one draw needn't show every extreme that they name: `tile_live`: each aligned block of 2 x 4 tiles (the tiles of one device) holds 1 to 4 live tiles, exactly 4 in some block; every diagonal tile is live. `prune_keep`: every diagonal entry is 1.
All inputs are finite; a program needn't handle non-finite values.
Results may differ from the reference program's by a relative error of at most 0.0003.
Values may be sent and summed in bfloat16 or wider, within the bound.
No kernel may reach another device: no remote copies, remote signals or barrier semaphores. Data moves between devices by JAX's collectives and lax.ppermute only.
A program may use at most 128 MiB of HBM per device.

```python
import math
import jax
import jax.numpy as jnp
from jax import lax

TILE = 128
RT = 2
LIVE = 4
NT = 64
CT = 4
NODES = 8192
N_COL = 16


def draw_tile_live(key, part):
    key = jax.random.fold_in(key, 7)
    key_count, key_pick, key_score = jax.random.split(key, 3)
    block_rows = NT // RT
    block_cols = NT // CT
    inside = RT * CT
    counts = jax.random.randint(key_count, (block_rows * block_cols,), 1, LIVE + 1)
    chosen = jax.random.randint(key_pick, (), 0, block_rows * block_cols)
    counts = jnp.where(jnp.arange(block_rows * block_cols) == chosen, LIVE, counts)
    counts = counts.reshape(block_rows, block_cols)
    diagonal = (jnp.arange(NT)[:, None] == jnp.arange(NT)[None, :]).astype(jnp.int32)
    diagonal = diagonal.reshape(block_rows, RT, block_cols, CT).transpose(0, 2, 1, 3).reshape(block_rows, block_cols, inside)
    position = jnp.arange(inside, dtype=jnp.int32)[None, None, :]
    scores = jax.random.randint(key_score, (block_rows, block_cols, inside), 0, 1 << 20)
    keyed = jnp.where(diagonal > 0, position, (scores + 1) * inside + position)
    ranks = jnp.argsort(jnp.argsort(keyed, axis=2), axis=2)
    needed = jnp.maximum(counts, jnp.sum(diagonal, axis=2))
    live = (ranks < needed[:, :, None]).astype(jnp.int32)
    return live.reshape(block_rows, block_cols, RT, CT).transpose(0, 2, 1, 3).reshape(NT, NT)


def draw_prune_keep(key, part):
    key = jax.random.fold_in(key, 11)
    levels = jax.random.randint(key, (NODES, NODES), 0, 4)
    diagonal = jnp.arange(NODES)[:, None] == jnp.arange(NODES)[None, :]
    return jnp.where(diagonal | (levels > 0), 1, 0).astype(jnp.int32)


def steps_of(stream_key, shape, pieces, smallest, high):
    factor_of = 1.0
    for dim, blocks in pieces:
        heights = jax.random.uniform(jax.random.fold_in(jax.random.fold_in(stream_key, 6), dim), (blocks,), jnp.float32, smallest / len(pieces), high / len(pieces))
        factor_of = factor_of * jnp.repeat(jnp.exp(heights), shape[dim] // blocks).reshape((-1,) + (1,) * (len(shape) - 1 - dim))
    return factor_of


def setup_inputs(seed: int = 0) -> dict:
    keys = jax.random.split(jax.random.key(seed), 4)
    return {
        "transition": jnp.clip(jnp.exp(math.log(1.0) - 4.61031033 * jax.random.uniform(keys[0], (NODES, NODES), jnp.float32) ** steps_of(keys[0], (NODES, NODES), ((0, 32), (1, 16)), -0.2, 0.2)), 0.0099487305, 1.0).astype(jnp.bfloat16),
        "tile_live": draw_tile_live(jax.random.fold_in(keys[3], 71), 0),
        "prune_keep": draw_prune_keep(jax.random.fold_in(keys[3], 71), 0),
    }


def reference(transition, tile_live, prune_keep):
    live_cells = jnp.repeat(jnp.repeat(tile_live, TILE, axis=0), TILE, axis=1)
    masked = transition * live_cells.astype(jnp.bfloat16)
    widened = masked.astype(jnp.float32)
    expanded = jnp.dot(widened, widened, precision=lax.Precision.HIGHEST, preferred_element_type=jnp.float32)
    kept = expanded * prune_keep.astype(jnp.float32)
    inflated = kept * kept
    column_total = jnp.sum(inflated, axis=0)
    scaled = (NT * TILE) * inflated / column_total[None, :]
    return scaled.T.reshape(N_COL, CT * TILE, NT * TILE)
```

```python
import jax
import jax.numpy as jnp
from jax import lax
from jax.experimental import pallas as pl
from jax.experimental.pallas import tpu as pltpu
from jax.sharding import PartitionSpec as P

TILE = 128
LIVE = 4
UNIT = 16384.0
STEPS = 4


def spots(rows, cols):
    return [(a, b, slice(a * TILE, (a + 1) * TILE), slice(b * TILE, (b + 1) * TILE)) for a in range(rows) for b in range(cols)]


def pack_body(live, x_ref, out_ref):
    rows, cols = x_ref.shape[0] // TILE, x_ref.shape[1] // TILE
    top, left = lax.axis_index("row") * rows, lax.axis_index("col") * cols
    slot = jnp.int32(0)
    for a, b, across, down in spots(rows, cols):
        flag = live[top + a, left + b]

        @pl.when((flag > 0) & (slot < LIVE))
        def _(slot=slot, across=across, down=down):
            units = x_ref[across, down].astype(jnp.float32) * UNIT
            out_ref[slot] = units.astype(jnp.int32).astype(jnp.int16)

        slot = slot + flag


def pack(tile_live, transition):
    return pl.pallas_call(
        pack_body,
        out_shape=jax.ShapeDtypeStruct((LIVE, TILE, TILE), jnp.int16),
        in_specs=[pl.BlockSpec(memory_space=pltpu.SMEM), pl.BlockSpec(memory_space=pltpu.VMEM)],
        out_specs=pl.BlockSpec(memory_space=pltpu.VMEM),
        name="pack",
    )(tile_live, transition)


def unpack(live, top, left, rows, cols, slots_ref, group, dense_ref, base):
    slot = jnp.int32(0)
    for a, b, across, down in spots(rows, cols):
        flag = live[top + a, left + b]
        tile = slots_ref[group, jnp.minimum(slot, LIVE - 1)].astype(jnp.float32)
        tile = jnp.where(flag > 0, tile, 0.0).astype(jnp.bfloat16)
        dense_ref[base + a * TILE : base + (a + 1) * TILE, down] = tile
        slot = slot + flag


def product_body(rows, cols, live, a_ref, b_ref, keep_ref, out_ref, a_dense, b_dense, total):
    step = pl.program_id(0)
    per = a_ref.shape[0]
    each = b_ref.shape[0] // per
    top, left = lax.axis_index("row") * rows, lax.axis_index("col") * cols

    @pl.when(step == 0)
    def _():
        total[...] = jnp.zeros_like(total)

    for p in range(per):
        panel = step * per + p
        unpack(live, top, panel * cols, rows, cols, a_ref, p, a_dense.at[p % 2], 0)
        for e in range(each):
            unpack(live, (panel * each + e) * rows, left, rows, cols, b_ref, p * each + e, b_dense.at[p % 2], e * rows * TILE)
        total[...] += jnp.dot(a_dense[p % 2], b_dense[p % 2], preferred_element_type=jnp.float32)

    @pl.when(step == pl.num_programs(0) - 1)
    def _():
        kept = total[...] * (keep_ref[...].astype(jnp.float32) * (1.0 / (UNIT * UNIT)))
        inflated = (kept * kept).T
        out_ref[...] = inflated.reshape(out_ref.shape)


def product(tile_live, row_panel, col_panel, keep):
    n_row, n_col = col_panel.shape[0], row_panel.shape[0]
    height, width = keep.shape
    rows, cols = height // TILE, width // TILE
    per = n_col // STEPS
    each = width // height
    return pl.pallas_call(
        lambda *refs: product_body(rows, cols, *refs),
        out_shape=jax.ShapeDtypeStruct((n_row, width // n_row, height), jnp.float32),
        grid=(STEPS,),
        in_specs=[
            pl.BlockSpec(memory_space=pltpu.SMEM),
            pl.BlockSpec((per, LIVE, TILE, TILE), lambda s: (s, 0, 0, 0)),
            pl.BlockSpec((per * each, LIVE, TILE, TILE), lambda s: (s, 0, 0, 0)),
            pl.BlockSpec((height, width), lambda s: (0, 0)),
        ],
        out_specs=pl.BlockSpec((n_row, width // n_row, height), lambda s: (0, 0, 0)),
        scratch_shapes=[
            pltpu.VMEM((2, height, width), jnp.bfloat16),
            pltpu.VMEM((2, width, width), jnp.bfloat16),
            pltpu.VMEM((height, width), jnp.float32),
        ],
        compiler_params=pltpu.CompilerParams(dimension_semantics=("arbitrary",), vmem_limit_bytes=32 * 1024 * 1024),
        name="product",
    )(tile_live, row_panel, col_panel, keep)


def scale_body(x_ref, out_ref):
    parts, _, height = x_ref.shape
    nodes = parts * height
    entries = x_ref[...]
    column_total = jnp.sum(jnp.sum(entries, axis=0), axis=1, keepdims=True)
    factor = nodes / column_total
    for p in range(parts):
        out_ref[0, :, p * height : (p + 1) * height] = entries[p] * factor


def scale(entries):
    parts, strips, height = entries.shape
    return pl.pallas_call(
        scale_body,
        out_shape=jax.ShapeDtypeStruct((1, strips, parts * height), jnp.float32),
        in_specs=[pl.BlockSpec(memory_space=pltpu.VMEM)],
        out_specs=pl.BlockSpec(memory_space=pltpu.VMEM),
        name="scale",
    )(entries)


def shards(transition, tile_live, prune_keep):
    packed = pack(tile_live, transition)
    row_panel = lax.all_gather(packed, "col", axis=0)
    col_panel = lax.all_gather(packed, "row", axis=0)
    strips = product(tile_live, row_panel, col_panel, prune_keep)
    entries = lax.all_to_all(strips, "row", split_axis=0, concat_axis=0, tiled=True)
    return scale(entries)


def solution(mesh):
    placed = (P("row", "col"), P(), P("row", "col"))
    return jax.shard_map(
        shards, mesh=mesh, in_specs=placed, out_specs=P("col", "row", None), check_vma=False
    )
```

```python
import jax
import jax.numpy as jnp
from jax import lax
from jax.experimental import pallas as pl
from jax.experimental.pallas import tpu as pltpu
from jax.sharding import PartitionSpec as P

TILE = 128
LIVE = 4
UNIT = 16384.0
X, Y, CORES = 4, 4, 2


def spots(rows, cols):
    return [(a, b, slice(a * TILE, (a + 1) * TILE), slice(b * TILE, (b + 1) * TILE)) for a in range(rows) for b in range(cols)]


def pack_body(live, x_ref, out_ref):
    rows, cols = x_ref.shape[0] // TILE, x_ref.shape[1] // TILE
    top, left = lax.axis_index("row") * rows, lax.axis_index("col") * cols
    slot = jnp.int32(0)
    for a, b, across, down in spots(rows, cols):
        flag = live[top + a, left + b]

        @pl.when((flag > 0) & (slot < LIVE))
        def _(slot=slot, across=across, down=down):
            units = x_ref[across, down].astype(jnp.float32) * UNIT
            out_ref[slot] = units.astype(jnp.int32).astype(jnp.int16)

        slot = slot + flag


def pack(tile_live, transition):
    return pl.pallas_call(
        pack_body,
        out_shape=jax.ShapeDtypeStruct((LIVE, TILE, TILE), jnp.int16),
        in_specs=[pl.BlockSpec(memory_space=pltpu.SMEM), pl.BlockSpec(memory_space=pltpu.VMEM)],
        out_specs=pl.BlockSpec(memory_space=pltpu.VMEM),
        name="pack",
    )(tile_live, transition)


def unpack(live, top, left, rows, cols, slots_ref, group, dense_ref, base):
    slot = jnp.int32(0)
    for a, b, across, down in spots(rows, cols):
        flag = live[top + a, left + b]
        tile = slots_ref[group, jnp.minimum(slot, LIVE - 1)].astype(jnp.float32)
        tile = jnp.where(flag > 0, tile, 0.0).astype(jnp.bfloat16)
        dense_ref[base + a * TILE : base + (a + 1) * TILE, down] = tile
        slot = slot + flag


def product_body(rows, cols, live, a_ref, b_ref, keep_ref, out_ref, a_dense, b_dense, total):
    y = pl.program_id(0)
    place = lax.axis_index("row")
    top, left = place * rows, lax.axis_index("col") * cols
    x = place // (Y * CORES)

    @pl.when(y == 0)
    def _():
        total[...] = jnp.zeros_like(total)

    for back in range(X):
        from_x = lax.rem(x + X - back, X)
        panel = from_x * Y + y
        unpack(live, top, panel * cols, rows, cols, a_ref.at[:, 0], from_x, a_dense.at[back % 2], 0)
        for e in range(CORES):
            unpack(live, (panel * CORES + e) * rows, left, rows, cols, b_ref.at[:, back, 0], e, b_dense.at[back % 2], e * rows * TILE)
        total[...] += jnp.dot(a_dense[back % 2], b_dense[back % 2], preferred_element_type=jnp.float32)

    @pl.when(y == Y - 1)
    def _():
        kept = total[...] * (keep_ref[...].astype(jnp.float32) * (1.0 / (UNIT * UNIT)))
        inflated = (kept * kept).T
        out_ref[...] = inflated.reshape(out_ref.shape)


def product(tile_live, row_panel, col_panel, keep):
    n_row = X * Y * CORES
    height, width = keep.shape
    rows, cols = height // TILE, width // TILE
    return pl.pallas_call(
        lambda *refs: product_body(rows, cols, *refs),
        out_shape=jax.ShapeDtypeStruct((n_row, width // n_row, height), jnp.float32),
        grid=(Y,),
        in_specs=[
            pl.BlockSpec(memory_space=pltpu.SMEM),
            pl.BlockSpec((X, 1, LIVE, TILE, TILE), lambda y: (0, y, 0, 0, 0)),
            pl.BlockSpec((CORES, X, 1, LIVE, TILE, TILE), lambda y: (0, 0, y, 0, 0, 0)),
            pl.BlockSpec((height, width), lambda y: (0, 0)),
        ],
        out_specs=pl.BlockSpec((n_row, width // n_row, height), lambda y: (0, 0, 0)),
        scratch_shapes=[
            pltpu.VMEM((2, height, width), jnp.bfloat16),
            pltpu.VMEM((2, width, width), jnp.bfloat16),
            pltpu.VMEM((height, width), jnp.float32),
        ],
        compiler_params=pltpu.CompilerParams(dimension_semantics=("arbitrary",), vmem_limit_bytes=32 * 1024 * 1024),
        name="product",
    )(tile_live, row_panel.reshape(X, Y, LIVE, TILE, TILE), col_panel, keep)


def scale_body(x_ref, out_ref):
    parts, _, height = x_ref.shape
    nodes = parts * height
    entries = x_ref[...]
    column_total = jnp.sum(jnp.sum(entries, axis=0), axis=1, keepdims=True)
    factor = nodes / column_total
    for p in range(parts):
        out_ref[0, :, p * height : (p + 1) * height] = entries[p] * factor


def scale(entries):
    parts, strips, height = entries.shape
    return pl.pallas_call(
        scale_body,
        out_shape=jax.ShapeDtypeStruct((1, strips, parts * height), jnp.float32),
        in_specs=[pl.BlockSpec(memory_space=pltpu.VMEM)],
        out_specs=pl.BlockSpec(memory_space=pltpu.VMEM),
        name="scale",
    )(entries)


def row_place(x, y, core):
    return (x * Y + y) * CORES + core


def shards(transition, tile_live, prune_keep):
    along_y = [[row_place(x, y, c) for y in range(Y)] for x in range(X) for c in range(CORES)]
    pairs = [[row_place(x, y, c) for c in range(CORES)] for x in range(X) for y in range(Y)]
    ahead = [
        [(row_place(x, y, c), row_place((x + step) % X, y, c)) for x in range(X) for y in range(Y) for c in range(CORES)]
        for step in range(X)
    ]
    packed = pack(tile_live, transition)
    mine = lax.all_gather(packed, "row", axis=0, axis_index_groups=along_y)
    from_x = [mine] + [lax.ppermute(mine, "row", ahead[step]) for step in range(1, X)]
    row_panel = lax.all_gather(packed, "col", axis=0)
    col_panel = lax.all_gather(jnp.stack(from_x), "row", axis=0, axis_index_groups=pairs)
    strips = product(tile_live, row_panel, col_panel, prune_keep)
    entries = lax.all_to_all(strips, "row", split_axis=0, concat_axis=0, tiled=True)
    return scale(entries)


def solution(mesh):
    placed = (P("row", "col"), P(), P("row", "col"))
    return jax.shard_map(
        shards, mesh=mesh, in_specs=placed, out_specs=P("col", "row", None), check_vma=False
    )
```

```python
import jax
import jax.numpy as jnp
from jax import lax
from jax.experimental import pallas as pl
from jax.experimental.pallas import tpu as pltpu
from jax.sharding import PartitionSpec as P

TILE = 128
LIVE = 4
UNIT = 16384.0
X, Y, CORES = 4, 4, 2


def spots(rows, cols):
    half = cols // CORES
    return [(a, side * half + b) for side in range(CORES) for a in range(rows) for b in range(half)]


def tile_at(a, b):
    return slice(a * TILE, (a + 1) * TILE), slice(b * TILE, (b + 1) * TILE)


def pack_body(live, x_ref, out_ref):
    rows, cols = x_ref.shape[0] // TILE, x_ref.shape[1] // TILE
    top, left = lax.axis_index("row") * rows, lax.axis_index("col") * cols
    slot = jnp.int32(0)
    for a, b in spots(rows, cols):
        flag = live[top + a, left + b]

        @pl.when((flag > 0) & (slot < LIVE))
        def _(slot=slot, a=a, b=b):
            units = x_ref[tile_at(a, b)].astype(jnp.float32) * UNIT
            out_ref[slot] = units.astype(jnp.int32).astype(jnp.int16)

        slot = slot + flag


def pack(tile_live, transition):
    return pl.pallas_call(
        pack_body,
        out_shape=jax.ShapeDtypeStruct((LIVE, TILE, TILE), jnp.int16),
        in_specs=[pl.BlockSpec(memory_space=pltpu.SMEM), pl.BlockSpec(memory_space=pltpu.VMEM)],
        out_specs=pl.BlockSpec(memory_space=pltpu.VMEM),
        name="pack",
    )(tile_live, transition)


def unpack(live, top, left, places, slots_ref, slot, dense_ref, down, across):
    for a, b in places:
        flag = live[top + a, left + b]
        tile = slots_ref[jnp.minimum(slot, LIVE - 1)].astype(jnp.float32)
        tile = jnp.where(flag > 0, tile, 0.0).astype(jnp.bfloat16)
        dense_ref[down + a * TILE : down + (a + 1) * TILE, across + b * TILE : across + (b + 1) * TILE] = tile
        slot = slot + flag


def half_body(other, rows, cols, live, a_ref, b_ref, *refs):
    if other:
        before_ref, keep_ref, out_ref, a_dense, b_dense, total = refs
    else:
        out_ref, a_dense, b_dense = refs
        total = out_ref
    place = lax.axis_index("row")
    top, left = place * rows, lax.axis_index("col") * cols
    x, y = place // (Y * CORES), lax.rem(place // CORES, Y)
    side = lax.rem(place, CORES)
    if other:
        side = 1 - side
    half = cols // CORES
    total[...] = before_ref[...] if other else jnp.zeros_like(total)

    @pl.loop(0, X)
    def _(back_x):
        for back_y in range(Y):
            panel = lax.rem(x + X - back_x, X) * Y + lax.rem(y + Y - back_y, Y)
            first = sum(live[top + a, panel * cols + b] for a in range(rows) for b in range(half))
            unpack(
                live, top, panel * cols + side * half, [(a, b) for a in range(rows) for b in range(half)],
                a_ref.at[panel], side * first, a_dense, 0, back_y * half * TILE,
            )
            unpack(
                live, (panel * CORES + side) * rows, left, spots(rows, cols),
                b_ref.at[back_x, back_y], jnp.int32(0), b_dense, back_y * rows * TILE, 0,
            )
        total[...] += jnp.dot(a_dense[...], b_dense[...], preferred_element_type=jnp.float32)

    if other:
        kept = total[...] * (keep_ref[...].astype(jnp.float32) * (1.0 / (UNIT * UNIT)))
        inflated = (kept * kept).T
        out_ref[...] = inflated.reshape(out_ref.shape)


def half_product(tile_live, row_panel, col_half, *rest):
    n_row = X * Y * CORES
    height, width = TILE * tile_live.shape[0] // n_row, TILE * tile_live.shape[1] // row_panel.shape[0]
    rows, cols = height // TILE, width // TILE
    other = bool(rest)
    out = (n_row, width // n_row, height) if other else (height, width)
    depth = Y * height
    in_vmem = pl.BlockSpec(memory_space=pltpu.VMEM)
    return pl.pallas_call(
        lambda *refs: half_body(other, rows, cols, *refs),
        out_shape=jax.ShapeDtypeStruct(out, jnp.float32),
        in_specs=[pl.BlockSpec(memory_space=pltpu.SMEM), in_vmem, in_vmem, *[in_vmem for _ in rest]],
        out_specs=in_vmem,
        scratch_shapes=[
            pltpu.VMEM((height, depth), jnp.bfloat16),
            pltpu.VMEM((depth, width), jnp.bfloat16),
        ] + [pltpu.VMEM((height, width), jnp.float32)] * other,
        compiler_params=pltpu.CompilerParams(vmem_limit_bytes=24 * 1024 * 1024),
        cost_estimate=pl.CostEstimate(flops=2 * height * depth * X * width, bytes_accessed=5 * 1024 * 1024, transcendentals=0),
        name="other_half" if other else "own_half",
    )(tile_live, row_panel, col_half, *rest)


def scale_body(x_ref, out_ref):
    parts, _, height = x_ref.shape
    nodes = parts * height
    entries = x_ref[...]
    column_total = jnp.sum(jnp.sum(entries, axis=0), axis=1, keepdims=True)
    factor = nodes / column_total
    for p in range(parts):
        out_ref[0, :, p * height : (p + 1) * height] = entries[p] * factor


def scale(entries):
    parts, strips, height = entries.shape
    return pl.pallas_call(
        scale_body,
        out_shape=jax.ShapeDtypeStruct((1, strips, parts * height), jnp.float32),
        in_specs=[pl.BlockSpec(memory_space=pltpu.VMEM)],
        out_specs=pl.BlockSpec(memory_space=pltpu.VMEM),
        name="scale",
    )(entries)


def row_place(x, y, core):
    return (x % X * Y + y % Y) * CORES + core % CORES


def moved(part, x=0, y=0, core=0):
    hops = [
        (row_place(i, j, k), row_place(i + x, j + y, k + core)) for i in range(X) for j in range(Y) for k in range(CORES)
    ]
    return lax.ppermute(part, "row", hops)


def shards(transition, tile_live, prune_keep):
    packed = pack(tile_live, transition)
    around = jnp.stack([packed] + [moved(packed, y=step) for step in range(1, Y)])
    own = [around] + [moved(around, x=step) for step in range(1, X)]
    row_panel = lax.all_gather(packed, "col", axis=0)
    own = jnp.stack(own) + jnp.minimum(row_panel[0, 0, 0, 0], 0)
    other = moved(own, core=1)
    total = half_product(tile_live, row_panel, own)
    strips = half_product(tile_live, row_panel, other, total, prune_keep)
    entries = lax.all_to_all(strips, "row", split_axis=0, concat_axis=0, tiled=True)
    return scale(entries)


def solution(mesh):
    placed = (P("row", "col"), P(), P("row", "col"))
    return jax.shard_map(
        shards, mesh=mesh, in_specs=placed, out_specs=P("col", "row", None), check_vma=False
    )
```

```python
import jax
import jax.numpy as jnp
from jax import lax
from jax.experimental import pallas as pl
from jax.experimental.pallas import tpu as pltpu
from jax.sharding import PartitionSpec as P

TILE = 128
LIVE = 4
UNIT = 16384.0
STEPS = 4


def spots(rows, cols):
    return [(a, b, slice(a * TILE, (a + 1) * TILE), slice(b * TILE, (b + 1) * TILE)) for a in range(rows) for b in range(cols)]


def pack_body(live, x_ref, units_ref, plain_ref):
    rows, cols = x_ref.shape[0] // TILE, x_ref.shape[1] // TILE
    top, left = lax.axis_index("row") * rows, lax.axis_index("col") * cols
    slot = jnp.int32(0)
    for a, b, across, down in spots(rows, cols):
        flag = live[top + a, left + b]

        @pl.when((flag > 0) & (slot < LIVE))
        def _(slot=slot, across=across, down=down):
            tile = x_ref[across, down]
            plain_ref[slot] = tile
            units_ref[slot] = (tile.astype(jnp.float32) * UNIT).astype(jnp.int32).astype(jnp.int16)

        slot = slot + flag


def pack(tile_live, transition):
    in_vmem = pl.BlockSpec(memory_space=pltpu.VMEM)
    slots = (LIVE, TILE, TILE)
    return pl.pallas_call(
        pack_body,
        out_shape=[jax.ShapeDtypeStruct(slots, jnp.int16), jax.ShapeDtypeStruct(slots, transition.dtype)],
        in_specs=[pl.BlockSpec(memory_space=pltpu.SMEM), in_vmem],
        out_specs=[in_vmem, in_vmem],
        name="pack",
    )(tile_live, transition)


def unpack(live, top, left, rows, cols, slots_ref, group, dense_ref, height, width):
    slot = jnp.int32(0)
    for a, b, _, _ in spots(rows, cols):
        flag = live[top + a, left + b]
        tile = slots_ref[group, jnp.minimum(slot, LIVE - 1)]
        tile = jnp.where(flag > 0, tile, jnp.zeros_like(tile))
        if tile.dtype != dense_ref.dtype:
            tile = tile.astype(jnp.float32).astype(dense_ref.dtype)
        dense_ref[height + a * TILE : height + (a + 1) * TILE, width + b * TILE : width + (b + 1) * TILE] = tile
        slot = slot + flag


def spread_body(rows, cols, live, a_ref, out_ref):
    step = pl.program_id(0)
    per = a_ref.shape[0]
    top = lax.axis_index("row") * rows
    for p in range(per):
        unpack(live, top, (step * per + p) * cols, rows, cols, a_ref, p, out_ref.at[0], 0, p * cols * TILE)


def spread(tile_live, row_panel, height, width):
    per = row_panel.shape[0] // STEPS
    rows, cols = height // TILE, width // TILE
    return pl.pallas_call(
        lambda *refs: spread_body(rows, cols, *refs),
        out_shape=jax.ShapeDtypeStruct((STEPS, height, per * width), jnp.bfloat16),
        grid=(STEPS,),
        in_specs=[
            pl.BlockSpec(memory_space=pltpu.SMEM),
            pl.BlockSpec((per, LIVE, TILE, TILE), lambda s: (s, 0, 0, 0)),
        ],
        out_specs=pl.BlockSpec((1, height, per * width), lambda s: (s, 0, 0)),
        cost_estimate=pl.CostEstimate(flops=0, bytes_accessed=6 * 1024 * 1024, transcendentals=0),
        name="spread",
    )(tile_live, row_panel)


def product_body(rows, cols, live, a_ref, b_ref, keep_ref, out_ref, b_dense, total):
    step = pl.program_id(0)
    per = b_ref.shape[0]
    left = lax.axis_index("col") * cols
    for p in range(per):
        unpack(live, (step * per + p) * rows, left, rows, cols, b_ref, p, b_dense, p * rows * TILE, 0)
    part = jnp.dot(a_ref[0], b_dense[...], preferred_element_type=jnp.float32)

    @pl.when(step == 0)
    def _():
        total[...] = part

    @pl.when(step > 0)
    def _():
        total[...] += part

    @pl.when(step == pl.num_programs(0) - 1)
    def _():
        kept = total[...] * (keep_ref[...].astype(jnp.float32) * (1.0 / UNIT))
        inflated = (kept * kept).T
        out_ref[...] = inflated.reshape(out_ref.shape)


def product(tile_live, row_panel, col_panel, keep):
    n_row, depth = col_panel.shape[0], row_panel.shape[2]
    height, width = keep.shape
    rows, cols = height // TILE, width // TILE
    return pl.pallas_call(
        lambda *refs: product_body(rows, cols, *refs),
        out_shape=jax.ShapeDtypeStruct((n_row, width // n_row, height), jnp.float32),
        grid=(STEPS,),
        in_specs=[
            pl.BlockSpec(memory_space=pltpu.SMEM),
            pl.BlockSpec((1, height, depth), lambda s: (s, 0, 0)),
            pl.BlockSpec((n_row // STEPS, LIVE, TILE, TILE), lambda s: (s, 0, 0, 0)),
            pl.BlockSpec((height, width), lambda s: (0, 0)),
        ],
        out_specs=pl.BlockSpec((n_row, width // n_row, height), lambda s: (0, 0, 0)),
        scratch_shapes=[
            pltpu.VMEM((depth, width), jnp.bfloat16),
            pltpu.VMEM((height, width), jnp.float32),
        ],
        compiler_params=pltpu.CompilerParams(dimension_semantics=("arbitrary",), vmem_limit_bytes=56 * 1024 * 1024),
        name="product",
    )(tile_live, row_panel, col_panel, keep)


def scale_body(x_ref, out_ref):
    parts, _, height = x_ref.shape
    nodes = parts * height
    entries = x_ref[...]
    column_total = jnp.sum(jnp.sum(entries, axis=0), axis=1, keepdims=True)
    factor = nodes / column_total
    for p in range(parts):
        out_ref[0, :, p * height : (p + 1) * height] = entries[p] * factor


def scale(entries):
    parts, strips, height = entries.shape
    return pl.pallas_call(
        scale_body,
        out_shape=jax.ShapeDtypeStruct((1, strips, parts * height), jnp.float32),
        in_specs=[pl.BlockSpec(memory_space=pltpu.VMEM)],
        out_specs=pl.BlockSpec(memory_space=pltpu.VMEM),
        name="scale",
    )(entries)


def shards(transition, tile_live, prune_keep):
    units, plain = pack(tile_live, transition)
    col_panel = lax.all_gather(plain, "row", axis=0)
    row_panel = lax.all_gather(units, "col", axis=0)
    row_panel = spread(tile_live, row_panel, *transition.shape)
    strips = product(tile_live, row_panel, col_panel, prune_keep)
    entries = lax.all_to_all(strips, "row", split_axis=0, concat_axis=0, tiled=True)
    return scale(entries)


def solution(mesh):
    placed = (P("row", "col"), P(), P("row", "col"))
    return jax.shard_map(
        shards, mesh=mesh, in_specs=placed, out_specs=P("col", "row", None), check_vma=False
    )
```

```python
import jax
import jax.numpy as jnp
from jax import lax
from jax.experimental import pallas as pl
from jax.experimental.pallas import tpu as pltpu
from jax.sharding import PartitionSpec as P

TILE = 128
LIVE = 4
UNIT = 16384.0
PARTS = 2


def spots(rows, cols):
    return [(a, b, slice(a * TILE, (a + 1) * TILE), slice(b * TILE, (b + 1) * TILE)) for a in range(rows) for b in range(cols)]


def pack_body(live, x_ref, out_ref):
    rows, cols = x_ref.shape[0] // TILE, x_ref.shape[1] // TILE
    top, left = lax.axis_index("row") * rows, lax.axis_index("col") * cols
    slot = jnp.int32(0)
    for a, b, across, down in spots(rows, cols):
        flag = live[top + a, left + b]

        @pl.when((flag > 0) & (slot < LIVE))
        def _(slot=slot, across=across, down=down):
            units = x_ref[across, down].astype(jnp.float32).T * UNIT
            out_ref[slot] = units.astype(jnp.int32).astype(jnp.int16)

        slot = slot + flag


def pack(tile_live, transition):
    return pl.pallas_call(
        pack_body,
        out_shape=jax.ShapeDtypeStruct((LIVE, TILE, TILE), jnp.int16),
        in_specs=[pl.BlockSpec(memory_space=pltpu.SMEM), pl.BlockSpec(memory_space=pltpu.VMEM)],
        out_specs=pl.BlockSpec(memory_space=pltpu.VMEM),
        name="pack",
    )(tile_live, transition)


def placing(live, top, left, rows, cols, slots_ref, dense_ref, down, across):
    slot, tasks = jnp.int32(0), []
    for spot, (a, b, _, _) in enumerate(spots(rows, cols)):
        flag = live[top + a, left + b]

        def place(flag=flag, slot=slot if spot < LIVE else jnp.minimum(slot, LIVE - 1), a=a, b=b):
            tile = slots_ref[slot].astype(jnp.float32)
            tile = jnp.where(flag > 0, tile, 0.0).astype(jnp.bfloat16)
            dense_ref[down + b * TILE : down + (b + 1) * TILE, across + a * TILE : across + (a + 1) * TILE] = tile

        tasks.append(place)
        slot = slot + flag
    return tasks


def product_body(rows, cols, live, a_ref, b_ref, keep_ref, out_ref, a_dense, b_dense, total):
    panels = a_ref.shape[0]
    each = b_ref.shape[0] // panels
    top, left = lax.axis_index("row") * rows, lax.axis_index("col") * cols

    def tasks_of(panel):
        a_to, b_to = a_dense.at[panel % 2], b_dense.at[panel % 2]
        tasks = placing(live, top, panel * cols, rows, cols, a_ref.at[panel], a_to, 0, 0)
        for e in range(each):
            group = panel * each + e
            tasks += placing(live, group * rows, left, rows, cols, b_ref.at[group], b_to, 0, e * rows * TILE)
        return tasks

    keep = keep_ref[...].astype(jnp.float32).T * (1.0 / (UNIT * UNIT))
    for place in tasks_of(0):
        place()
    for panel in range(panels):
        later = tasks_of(panel + 1) if panel + 1 < panels else []
        share, high = len(later) // PARTS, total.shape[0] // PARTS
        for part in range(PARTS):
            lines = slice(part * high, (part + 1) * high)
            product = jnp.dot(
                b_dense[panel % 2, lines, :], a_dense[panel % 2], preferred_element_type=jnp.float32
            )
            total[lines, :] = product if panel == 0 else total[lines, :] + product
            for place in later[part * share : (part + 1) * share]:
                place()
    kept = total[...] * keep
    out_ref[...] = (kept * kept).reshape(out_ref.shape)


def product(tile_live, row_panel, col_panel, keep):
    n_row = col_panel.shape[0]
    height, width = keep.shape
    rows, cols = height // TILE, width // TILE
    in_vmem = pl.BlockSpec(memory_space=pltpu.VMEM)
    return pl.pallas_call(
        lambda *refs: product_body(rows, cols, *refs),
        out_shape=jax.ShapeDtypeStruct((n_row, width // n_row, height), jnp.float32),
        in_specs=[pl.BlockSpec(memory_space=pltpu.SMEM), in_vmem, in_vmem, in_vmem],
        out_specs=in_vmem,
        scratch_shapes=[
            pltpu.VMEM((2, width, height), jnp.bfloat16),
            pltpu.VMEM((2, width, width), jnp.bfloat16),
            pltpu.VMEM((width, height), jnp.float32),
        ],
        compiler_params=pltpu.CompilerParams(vmem_limit_bytes=32 * 1024 * 1024),
        name="product",
    )(tile_live, row_panel, col_panel, keep)


def scale_body(x_ref, out_ref):
    parts, _, height = x_ref.shape
    nodes = parts * height
    entries = x_ref[...]
    column_total = jnp.sum(jnp.sum(entries, axis=0), axis=1, keepdims=True)
    factor = nodes / column_total
    for p in range(parts):
        out_ref[0, :, p * height : (p + 1) * height] = entries[p] * factor


def scale(entries):
    parts, strips, height = entries.shape
    return pl.pallas_call(
        scale_body,
        out_shape=jax.ShapeDtypeStruct((1, strips, parts * height), jnp.float32),
        in_specs=[pl.BlockSpec(memory_space=pltpu.VMEM)],
        out_specs=pl.BlockSpec(memory_space=pltpu.VMEM),
        name="scale",
    )(entries)


def shards(transition, tile_live, prune_keep):
    packed = pack(tile_live, transition)
    row_panel = lax.all_gather(packed, "col", axis=0)
    col_panel = lax.all_gather(packed, "row", axis=0)
    strips = product(tile_live, row_panel, col_panel, prune_keep)
    entries = lax.all_to_all(strips, "row", split_axis=0, concat_axis=0, tiled=True)
    return scale(entries)


def solution(mesh):
    placed = (P("row", "col"), P(), P("row", "col"))
    return jax.shard_map(
        shards, mesh=mesh, in_specs=placed, out_specs=P("col", "row", None), check_vma=False
    )
```

```python
import jax
import jax.numpy as jnp
from jax import lax
from jax.experimental import pallas as pl
from jax.experimental.pallas import tpu as pltpu
from jax.sharding import PartitionSpec as P

TILE = 128
LIVE = 4
UNIT = 16384.0
PARTS = 2
GROUP = 8


def spots(rows, cols):
    return [(a, b, slice(a * TILE, (a + 1) * TILE), slice(b * TILE, (b + 1) * TILE)) for a in range(rows) for b in range(cols)]


def pack_body(live_hbm, x_hbm, out_ref, live, x_ref, arrived):
    rows, cols = x_ref.shape[0] // TILE, x_ref.shape[1] // TILE
    top, left = lax.axis_index("row") * rows, lax.axis_index("col") * cols
    group = pl.multiple_of(top // GROUP * GROUP, GROUP)
    flags_in = pltpu.make_async_copy(live_hbm.at[pl.ds(group, GROUP)], live, arrived.at[0])
    block_in = pltpu.make_async_copy(x_hbm, x_ref, arrived.at[1])
    flags_in.start()
    block_in.start()
    flags_in.wait()
    block_in.wait()
    top = top - group
    slot = jnp.int32(0)
    for a, b, across, down in spots(rows, cols):
        flag = live[top + a, left + b]

        @pl.when((flag > 0) & (slot < LIVE))
        def _(slot=slot, across=across, down=down):
            units = x_ref[across, down].astype(jnp.float32).T * UNIT
            out_ref[slot] = units.astype(jnp.int32).astype(jnp.int16)

        slot = slot + flag


def pack(tile_live, transition):
    return pl.pallas_call(
        pack_body,
        out_shape=jax.ShapeDtypeStruct((LIVE, TILE, TILE), jnp.int16),
        in_specs=[pl.BlockSpec(memory_space=pl.ANY)] * 2,
        out_specs=pl.BlockSpec(memory_space=pltpu.VMEM),
        scratch_shapes=[
            pltpu.SMEM((GROUP, tile_live.shape[1]), tile_live.dtype),
            pltpu.VMEM(transition.shape, transition.dtype),
            pltpu.SemaphoreType.DMA((2,)),
        ],
        name="pack",
    )(tile_live, transition)


def placing(live, top, left, rows, cols, slots_ref, dense_ref, down, across):
    slot, tasks = jnp.int32(0), []
    for spot, (a, b, _, _) in enumerate(spots(rows, cols)):
        flag = live[top + a, left + b]

        def place(flag=flag, slot=slot if spot < LIVE else jnp.minimum(slot, LIVE - 1), a=a, b=b):
            tile = slots_ref[slot].astype(jnp.float32)
            tile = jnp.where(flag > 0, tile, 0.0).astype(jnp.bfloat16)
            dense_ref[down + b * TILE : down + (b + 1) * TILE, across + a * TILE : across + (a + 1) * TILE] = tile

        tasks.append(place)
        slot = slot + flag
    return tasks


def product_body(rows, cols, live_hbm, a_ref, b_ref, keep_ref, out_ref, live, a_dense, b_dense, total, arrived):
    flags_in = pltpu.make_async_copy(live_hbm, live, arrived)
    flags_in.start()
    panels = a_ref.shape[0]
    each = b_ref.shape[0] // panels
    top, left = lax.axis_index("row") * rows, lax.axis_index("col") * cols

    def tasks_of(panel):
        a_to, b_to = a_dense.at[panel % 2], b_dense.at[panel % 2]
        tasks = placing(live, top, panel * cols, rows, cols, a_ref.at[panel], a_to, 0, 0)
        for e in range(each):
            group = panel * each + e
            tasks += placing(live, group * rows, left, rows, cols, b_ref.at[group], b_to, 0, e * rows * TILE)
        return tasks

    keep = keep_ref[...].astype(jnp.float32).T * (1.0 / (UNIT * UNIT))
    flags_in.wait()
    for place in tasks_of(0):
        place()
    for panel in range(panels):
        later = tasks_of(panel + 1) if panel + 1 < panels else []
        share, high = len(later) // PARTS, total.shape[0] // PARTS
        for part in range(PARTS):
            lines = slice(part * high, (part + 1) * high)
            product = jnp.dot(
                b_dense[panel % 2, lines, :], a_dense[panel % 2], preferred_element_type=jnp.float32
            )
            total[lines, :] = product if panel == 0 else total[lines, :] + product
            for place in later[part * share : (part + 1) * share]:
                place()
    kept = total[...] * keep
    out_ref[...] = (kept * kept).reshape(out_ref.shape)


def product(tile_live, row_panel, col_panel, keep):
    n_row = col_panel.shape[0]
    height, width = keep.shape
    rows, cols = height // TILE, width // TILE
    in_vmem = pl.BlockSpec(memory_space=pltpu.VMEM)
    return pl.pallas_call(
        lambda *refs: product_body(rows, cols, *refs),
        out_shape=jax.ShapeDtypeStruct((n_row, width // n_row, height), jnp.float32),
        in_specs=[pl.BlockSpec(memory_space=pl.ANY), in_vmem, in_vmem, in_vmem],
        out_specs=in_vmem,
        scratch_shapes=[
            pltpu.SMEM(tile_live.shape, tile_live.dtype),
            pltpu.VMEM((2, width, height), jnp.bfloat16),
            pltpu.VMEM((2, width, width), jnp.bfloat16),
            pltpu.VMEM((width, height), jnp.float32),
            pltpu.SemaphoreType.DMA,
        ],
        compiler_params=pltpu.CompilerParams(vmem_limit_bytes=32 * 1024 * 1024),
        name="product",
    )(tile_live, row_panel, col_panel, keep)


def scale_body(x_ref, out_ref):
    parts, _, height = x_ref.shape
    nodes = parts * height
    entries = x_ref[...]
    column_total = jnp.sum(jnp.sum(entries, axis=0), axis=1, keepdims=True)
    factor = nodes / column_total
    for p in range(parts):
        out_ref[0, :, p * height : (p + 1) * height] = entries[p] * factor


def scale(entries):
    parts, strips, height = entries.shape
    return pl.pallas_call(
        scale_body,
        out_shape=jax.ShapeDtypeStruct((1, strips, parts * height), jnp.float32),
        in_specs=[pl.BlockSpec(memory_space=pltpu.VMEM)],
        out_specs=pl.BlockSpec(memory_space=pltpu.VMEM),
        compiler_params=pltpu.CompilerParams(vmem_limit_bytes=4 * 1024 * 1024),
        name="scale",
    )(entries)


def shards(transition, tile_live, prune_keep):
    packed = pack(tile_live, transition)
    row_panel = lax.all_gather(packed, "col", axis=0)
    col_panel = lax.all_gather(packed, "row", axis=0)
    strips = product(tile_live, row_panel, col_panel, prune_keep)
    entries = lax.all_to_all(strips, "row", split_axis=0, concat_axis=0, tiled=True)
    return scale(entries)


def solution(mesh):
    placed = (P("row", "col"), P(), P("row", "col"))
    return jax.shard_map(
        shards, mesh=mesh, in_specs=placed, out_specs=P("col", "row", None), check_vma=False
    )
```

```python
import jax
import jax.numpy as jnp
from jax import lax
from jax.experimental import pallas as pl
from jax.experimental.pallas import tpu as pltpu
from jax.sharding import PartitionSpec as P

TILE = 128
LIVE = 4
UNIT = 16384.0
PARTS = 2
GROUP = 8


def spots(rows, cols):
    return [(a, b, slice(a * TILE, (a + 1) * TILE), slice(b * TILE, (b + 1) * TILE)) for a in range(rows) for b in range(cols)]


def pack_body(live_hbm, x_hbm, out_ref, live, x_ref, arrived):
    rows, cols = x_ref.shape[0] // TILE, x_ref.shape[1] // TILE
    top, left = lax.axis_index("row") * rows, lax.axis_index("col") * cols
    group = pl.multiple_of(top // GROUP * GROUP, GROUP)
    flags_in = pltpu.make_async_copy(live_hbm.at[pl.ds(group, GROUP)], live, arrived.at[0])
    block_in = pltpu.make_async_copy(x_hbm, x_ref, arrived.at[1])
    flags_in.start()
    block_in.start()
    flags_in.wait()
    block_in.wait()
    top = top - group
    slot = jnp.int32(0)
    for a, b, across, down in spots(rows, cols):
        flag = live[top + a, left + b]

        @pl.when((flag > 0) & (slot < LIVE))
        def _(slot=slot, across=across, down=down):
            units = x_ref[across, down].astype(jnp.float32).T * UNIT
            out_ref[slot] = units.astype(jnp.int32).astype(jnp.int16)

        slot = slot + flag


def pack(tile_live, transition):
    return pl.pallas_call(
        pack_body,
        out_shape=jax.ShapeDtypeStruct((LIVE, TILE, TILE), jnp.int16),
        in_specs=[pl.BlockSpec(memory_space=pltpu.HBM)] * 2,
        out_specs=pl.BlockSpec(memory_space=pltpu.VMEM),
        scratch_shapes=[
            pltpu.SMEM((GROUP, tile_live.shape[1]), tile_live.dtype),
            pltpu.VMEM(transition.shape, transition.dtype),
            pltpu.SemaphoreType.DMA((2,)),
        ],
        compiler_params=pltpu.CompilerParams(vmem_limit_bytes=4 * 1024 * 1024),
        name="pack",
    )(tile_live, transition)


def placing(live, top, left, rows, cols, slots_ref, dense_ref, down, across):
    slot, tasks = jnp.int32(0), []
    for spot, (a, b, _, _) in enumerate(spots(rows, cols)):
        flag = live[top + a, left + b]

        def place(flag=flag, slot=slot if spot < LIVE else jnp.minimum(slot, LIVE - 1), a=a, b=b):
            tile = slots_ref[slot].astype(jnp.float32)
            tile = jnp.where(flag > 0, tile, 0.0).astype(jnp.bfloat16)
            dense_ref[down + b * TILE : down + (b + 1) * TILE, across + a * TILE : across + (a + 1) * TILE] = tile

        tasks.append(place)
        slot = slot + flag
    return tasks


def product_body(rows, cols, live_hbm, a_ref, b_ref, keep_ref, out_ref, live, a_dense, b_dense, total, arrived):
    flags_in = pltpu.make_async_copy(live_hbm, live, arrived)
    flags_in.start()
    panels = a_ref.shape[0]
    each = b_ref.shape[0] // panels
    top, left = lax.axis_index("row") * rows, lax.axis_index("col") * cols

    def tasks_of(panel):
        a_to, b_to = a_dense.at[panel % 2], b_dense.at[panel % 2]
        tasks = placing(live, top, panel * cols, rows, cols, a_ref.at[panel], a_to, 0, 0)
        for e in range(each):
            group = panel * each + e
            tasks += placing(live, group * rows, left, rows, cols, b_ref.at[group], b_to, 0, e * rows * TILE)
        return tasks

    keep = keep_ref[...].astype(jnp.float32).T * (1.0 / (UNIT * UNIT))
    flags_in.wait()
    for place in tasks_of(0):
        place()
    for panel in range(panels):
        later = tasks_of(panel + 1) if panel + 1 < panels else []
        share, high = len(later) // PARTS, total.shape[0] // PARTS
        for part in range(PARTS):
            lines = slice(part * high, (part + 1) * high)
            product = jnp.dot(
                b_dense[panel % 2, lines, :], a_dense[panel % 2], preferred_element_type=jnp.float32
            )
            total[lines, :] = product if panel == 0 else total[lines, :] + product
            for place in later[part * share : (part + 1) * share]:
                place()
    kept = total[...] * keep
    out_ref[...] = (kept * kept).reshape(out_ref.shape)


def product(tile_live, row_panel, col_panel, keep):
    n_row = col_panel.shape[0]
    height, width = keep.shape
    rows, cols = height // TILE, width // TILE
    in_vmem = pl.BlockSpec(memory_space=pltpu.VMEM)
    return pl.pallas_call(
        lambda *refs: product_body(rows, cols, *refs),
        out_shape=jax.ShapeDtypeStruct((n_row, width // n_row, height), jnp.float32),
        in_specs=[pl.BlockSpec(memory_space=pl.ANY), in_vmem, in_vmem, in_vmem],
        out_specs=in_vmem,
        scratch_shapes=[
            pltpu.SMEM(tile_live.shape, tile_live.dtype),
            pltpu.VMEM((2, width, height), jnp.bfloat16),
            pltpu.VMEM((2, width, width), jnp.bfloat16),
            pltpu.VMEM((width, height), jnp.float32),
            pltpu.SemaphoreType.DMA,
        ],
        compiler_params=pltpu.CompilerParams(vmem_limit_bytes=32 * 1024 * 1024),
        name="product",
    )(tile_live, row_panel, col_panel, keep)


def scale_body(x_ref, out_ref):
    parts, _, height = x_ref.shape
    nodes = parts * height
    entries = x_ref[...]
    column_total = jnp.sum(jnp.sum(entries, axis=0), axis=1, keepdims=True)
    factor = nodes / column_total
    for p in range(parts):
        out_ref[0, :, p * height : (p + 1) * height] = entries[p] * factor


def scale(entries):
    parts, strips, height = entries.shape
    return pl.pallas_call(
        scale_body,
        out_shape=jax.ShapeDtypeStruct((1, strips, parts * height), jnp.float32),
        in_specs=[pl.BlockSpec(memory_space=pltpu.VMEM)],
        out_specs=pl.BlockSpec(memory_space=pltpu.VMEM),
        compiler_params=pltpu.CompilerParams(vmem_limit_bytes=4 * 1024 * 1024),
        name="scale",
    )(entries)


def shards(transition, tile_live, prune_keep):
    packed = pack(tile_live, transition)
    row_panel = lax.all_gather(packed, "col", axis=0)
    col_panel = lax.all_gather(packed, "row", axis=0)
    strips = product(tile_live, row_panel, col_panel, prune_keep)
    entries = lax.all_to_all(strips, "row", split_axis=0, concat_axis=0, tiled=True)
    return scale(entries)


def solution(mesh):
    placed = (P("row", "col"), P(), P("row", "col"))
    return jax.shard_map(
        shards, mesh=mesh, in_specs=placed, out_specs=P("col", "row", None), check_vma=False
    )
```

```python
import jax
import jax.numpy as jnp
from jax import lax
from jax.experimental import pallas as pl
from jax.experimental.pallas import tpu as pltpu
from jax.sharding import PartitionSpec as P

TILE = 128
LIVE = 4
UNIT = 16384.0
LEVELS = 32700.0
OCTAVE = 0.6931471805599453 / 1024
SMALLEST = 2.0**-20
PARTS = 2
GROUP = 8


def spots(rows, cols):
    return [(a, b, slice(a * TILE, (a + 1) * TILE), slice(b * TILE, (b + 1) * TILE)) for a in range(rows) for b in range(cols)]


def pack_body(live_hbm, x_hbm, out_ref, live, x_ref, arrived):
    rows, cols = x_ref.shape[0] // TILE, x_ref.shape[1] // TILE
    top, left = lax.axis_index("row") * rows, lax.axis_index("col") * cols
    group = pl.multiple_of(top // GROUP * GROUP, GROUP)
    flags_in = pltpu.make_async_copy(live_hbm.at[pl.ds(group, GROUP)], live, arrived.at[0])
    block_in = pltpu.make_async_copy(x_hbm, x_ref, arrived.at[1])
    flags_in.start()
    block_in.start()
    flags_in.wait()
    block_in.wait()
    top = top - group
    slot = jnp.int32(0)
    for a, b, across, down in spots(rows, cols):
        flag = live[top + a, left + b]

        @pl.when((flag > 0) & (slot < LIVE))
        def _(slot=slot, across=across, down=down):
            units = x_ref[across, down].astype(jnp.float32).T * UNIT
            out_ref[slot] = units.astype(jnp.int32).astype(jnp.int16)

        slot = slot + flag


def pack(tile_live, transition):
    return pl.pallas_call(
        pack_body,
        out_shape=jax.ShapeDtypeStruct((LIVE, TILE, TILE), jnp.int16),
        in_specs=[pl.BlockSpec(memory_space=pl.ANY)] * 2,
        out_specs=pl.BlockSpec(memory_space=pltpu.VMEM),
        scratch_shapes=[
            pltpu.SMEM((GROUP, tile_live.shape[1]), tile_live.dtype),
            pltpu.VMEM(transition.shape, transition.dtype),
            pltpu.SemaphoreType.DMA((2,)),
        ],
        name="pack",
    )(tile_live, transition)


def placing(live, top, left, rows, cols, slots_ref, dense_ref, down, across):
    slot, tasks = jnp.int32(0), []
    for spot, (a, b, _, _) in enumerate(spots(rows, cols)):
        flag = live[top + a, left + b]

        def place(flag=flag, slot=slot if spot < LIVE else jnp.minimum(slot, LIVE - 1), a=a, b=b):
            tile = slots_ref[slot].astype(jnp.float32)
            tile = jnp.where(flag > 0, tile, 0.0).astype(jnp.bfloat16)
            dense_ref[down + b * TILE : down + (b + 1) * TILE, across + a * TILE : across + (a + 1) * TILE] = tile

        tasks.append(place)
        slot = slot + flag
    return tasks


def product_body(rows, cols, live_hbm, a_ref, b_ref, keep_ref, out_ref, live, a_dense, b_dense, total, arrived):
    flags_in = pltpu.make_async_copy(live_hbm, live, arrived)
    flags_in.start()
    panels = a_ref.shape[0]
    each = b_ref.shape[0] // panels
    top, left = lax.axis_index("row") * rows, lax.axis_index("col") * cols

    def tasks_of(panel):
        a_to, b_to = a_dense.at[panel % 2], b_dense.at[panel % 2]
        tasks = placing(live, top, panel * cols, rows, cols, a_ref.at[panel], a_to, 0, 0)
        for e in range(each):
            group = panel * each + e
            tasks += placing(live, group * rows, left, rows, cols, b_ref.at[group], b_to, 0, e * rows * TILE)
        return tasks

    keep = keep_ref[...].astype(jnp.float32).T * (1.0 / (UNIT * UNIT))
    flags_in.wait()
    for place in tasks_of(0):
        place()
    for panel in range(panels):
        later = tasks_of(panel + 1) if panel + 1 < panels else []
        share, high = len(later) // PARTS, total.shape[0] // PARTS
        for part in range(PARTS):
            lines = slice(part * high, (part + 1) * high)
            product = jnp.dot(
                b_dense[panel % 2, lines, :], a_dense[panel % 2], preferred_element_type=jnp.float32
            )
            total[lines, :] = product if panel == 0 else total[lines, :] + product
            for place in later[part * share : (part + 1) * share]:
                place()
    kept = total[...] * keep
    strips, height = out_ref.shape[:2], total.shape[1]
    largest = jnp.maximum(jnp.max(kept, axis=1, keepdims=True), SMALLEST)
    code = jnp.ceil(jnp.log(largest) * (1.0 / OCTAVE))
    levels = (kept * (LEVELS / jnp.exp(code * OCTAVE)) + 0.5).astype(jnp.int32).astype(jnp.int16)
    out_ref[:, :, :height] = levels.reshape(*strips, height)
    code = jnp.broadcast_to(code, (code.shape[0], TILE)).astype(jnp.int32).astype(jnp.int16)
    out_ref[:, :, height:] = code.reshape(*strips, TILE)


def product(tile_live, row_panel, col_panel, keep):
    n_row = col_panel.shape[0]
    height, width = keep.shape
    rows, cols = height // TILE, width // TILE
    in_vmem = pl.BlockSpec(memory_space=pltpu.VMEM)
    return pl.pallas_call(
        lambda *refs: product_body(rows, cols, *refs),
        out_shape=jax.ShapeDtypeStruct((n_row, width // n_row, height + TILE), jnp.int16),
        in_specs=[pl.BlockSpec(memory_space=pl.ANY), in_vmem, in_vmem, in_vmem],
        out_specs=in_vmem,
        scratch_shapes=[
            pltpu.SMEM(tile_live.shape, tile_live.dtype),
            pltpu.VMEM((2, width, height), jnp.bfloat16),
            pltpu.VMEM((2, width, width), jnp.bfloat16),
            pltpu.VMEM((width, height), jnp.float32),
            pltpu.SemaphoreType.DMA,
        ],
        compiler_params=pltpu.CompilerParams(vmem_limit_bytes=32 * 1024 * 1024),
        name="product",
    )(tile_live, row_panel, col_panel, keep)


def scale_body(x_ref, out_ref):
    parts, strips, height = x_ref.shape
    height = height - TILE
    nodes = parts * height
    unit = jnp.exp(x_ref[:, :, height:].astype(jnp.float32) * OCTAVE) * (1.0 / LEVELS)
    kept = [x_ref[:, :, at : at + TILE].astype(jnp.float32) * unit for at in range(0, height, TILE)]
    entries = jnp.concatenate([part * part for part in kept], axis=2)
    column_total = jnp.sum(jnp.sum(entries, axis=0), axis=1, keepdims=True)
    factor = nodes / column_total
    for p in range(parts):
        out_ref[0, :, p * height : (p + 1) * height] = entries[p] * factor


def scale(entries):
    parts, strips, height = entries.shape
    height = height - TILE
    return pl.pallas_call(
        scale_body,
        out_shape=jax.ShapeDtypeStruct((1, strips, parts * height), jnp.float32),
        in_specs=[pl.BlockSpec(memory_space=pltpu.VMEM)],
        out_specs=pl.BlockSpec(memory_space=pltpu.VMEM),
        compiler_params=pltpu.CompilerParams(vmem_limit_bytes=4 * 1024 * 1024),
        name="scale",
    )(entries)


def shards(transition, tile_live, prune_keep):
    packed = pack(tile_live, transition)
    row_panel = lax.all_gather(packed, "col", axis=0)
    col_panel = lax.all_gather(packed, "row", axis=0)
    strips = product(tile_live, row_panel, col_panel, prune_keep)
    entries = lax.all_to_all(strips, "row", split_axis=0, concat_axis=0, tiled=True)
    return scale(entries)


def solution(mesh):
    placed = (P("row", "col"), P(), P("row", "col"))
    return jax.shard_map(
        shards, mesh=mesh, in_specs=placed, out_specs=P("col", "row", None), check_vma=False
    )
```

```python
import jax
import jax.numpy as jnp
from jax import lax
from jax.experimental import pallas as pl
from jax.experimental.pallas import tpu as pltpu
from jax.sharding import PartitionSpec as P

TILE = 128
LIVE = 4
UNIT = 16384.0
LEVELS = 32700.0
OCTAVE = 0.6931471805599453 / 1024
SMALLEST = 2.0**-20
PARTS = 2
GROUP = 8


def spots(rows, cols):
    return [(a, b, slice(a * TILE, (a + 1) * TILE), slice(b * TILE, (b + 1) * TILE)) for a in range(rows) for b in range(cols)]


def pack_body(live_hbm, x_hbm, out_ref, live, x_ref, arrived):
    rows, cols = x_ref.shape[0] // TILE, x_ref.shape[1] // TILE
    top, left = lax.axis_index("row") * rows, lax.axis_index("col") * cols
    group = pl.multiple_of(top // GROUP * GROUP, GROUP)
    flags_in = pltpu.make_async_copy(live_hbm.at[pl.ds(group, GROUP)], live, arrived.at[0])
    block_in = pltpu.make_async_copy(x_hbm, x_ref, arrived.at[1])
    flags_in.start()
    block_in.start()
    flags_in.wait()
    block_in.wait()
    top = top - group
    slot = jnp.int32(0)
    for a, b, across, down in spots(rows, cols):
        flag = live[top + a, left + b]

        @pl.when((flag > 0) & (slot < LIVE))
        def _(slot=slot, across=across, down=down):
            units = x_ref[across, down].astype(jnp.float32).T * UNIT
            out_ref[slot] = units.astype(jnp.int32).astype(jnp.int16)

        slot = slot + flag


def pack(tile_live, transition):
    return pl.pallas_call(
        pack_body,
        out_shape=jax.ShapeDtypeStruct((LIVE, TILE, TILE), jnp.int16),
        in_specs=[pl.BlockSpec(memory_space=pl.ANY)] * 2,
        out_specs=pl.BlockSpec(memory_space=pltpu.VMEM),
        scratch_shapes=[
            pltpu.SMEM((GROUP, tile_live.shape[1]), tile_live.dtype),
            pltpu.VMEM(transition.shape, transition.dtype),
            pltpu.SemaphoreType.DMA((2,)),
        ],
        name="pack",
    )(tile_live, transition)


def placing(live, top, left, rows, cols, slots_ref, dense_ref, down, across):
    slot, tasks = jnp.int32(0), []
    for spot, (a, b, _, _) in enumerate(spots(rows, cols)):
        flag = live[top + a, left + b]

        def place(flag=flag, slot=slot if spot < LIVE else jnp.minimum(slot, LIVE - 1), a=a, b=b):
            tile = slots_ref[slot].astype(jnp.float32)
            tile = jnp.where(flag > 0, tile, 0.0).astype(jnp.bfloat16)
            dense_ref[down + b * TILE : down + (b + 1) * TILE, across + a * TILE : across + (a + 1) * TILE] = tile

        tasks.append(place)
        slot = slot + flag
    return tasks


def product_body(rows, cols, live_hbm, a_ref, b_ref, keep_ref, out_ref, live, a_dense, b_dense, total, arrived):
    flags_in = pltpu.make_async_copy(live_hbm, live, arrived)
    flags_in.start()
    panels = a_ref.shape[0]
    each = b_ref.shape[0] // panels
    top, left = lax.axis_index("row") * rows, lax.axis_index("col") * cols

    def tasks_of(panel):
        a_to, b_to = a_dense.at[panel % 2], b_dense.at[panel % 2]
        tasks = placing(live, top, panel * cols, rows, cols, a_ref.at[panel], a_to, 0, 0)
        for e in range(each):
            group = panel * each + e
            tasks += placing(live, group * rows, left, rows, cols, b_ref.at[group], b_to, 0, e * rows * TILE)
        return tasks

    keep = keep_ref[...].astype(jnp.float32).T * (1.0 / (UNIT * UNIT))
    flags_in.wait()
    for place in tasks_of(0):
        place()
    for panel in range(panels):
        later = tasks_of(panel + 1) if panel + 1 < panels else []
        share, high = len(later) // PARTS, total.shape[0] // PARTS
        for part in range(PARTS):
            lines = slice(part * high, (part + 1) * high)
            product = jnp.dot(
                b_dense[panel % 2, lines, :], a_dense[panel % 2], preferred_element_type=jnp.float32
            )
            total[lines, :] = product if panel == 0 else total[lines, :] + product
            for place in later[part * share : (part + 1) * share]:
                place()
    kept = total[...] * keep
    strips, height = out_ref.shape[:2], total.shape[1]
    largest = jnp.maximum(jnp.max(kept, axis=1, keepdims=True), SMALLEST)
    code = jnp.ceil(jnp.log(largest) * (1.0 / OCTAVE))
    levels = (kept * (LEVELS / jnp.exp(code * OCTAVE)) + 0.5).astype(jnp.int32).astype(jnp.int16)
    out_ref[:, :, :height] = levels.reshape(*strips, height)
    code = jnp.broadcast_to(code, (code.shape[0], TILE)).astype(jnp.int32).astype(jnp.int16)
    out_ref[:, :, height:] = code.reshape(*strips, TILE)


def product(tile_live, row_panel, col_panel, keep):
    n_row = col_panel.shape[0]
    height, width = keep.shape
    rows, cols = height // TILE, width // TILE
    in_vmem = pl.BlockSpec(memory_space=pltpu.VMEM)
    return pl.pallas_call(
        lambda *refs: product_body(rows, cols, *refs),
        out_shape=jax.ShapeDtypeStruct((n_row, width // n_row, height + TILE), jnp.int16),
        in_specs=[pl.BlockSpec(memory_space=pl.ANY), in_vmem, in_vmem, in_vmem],
        out_specs=in_vmem,
        scratch_shapes=[
            pltpu.SMEM(tile_live.shape, tile_live.dtype),
            pltpu.VMEM((2, width, height), jnp.bfloat16),
            pltpu.VMEM((2, width, width), jnp.bfloat16),
            pltpu.VMEM((width, height), jnp.float32),
            pltpu.SemaphoreType.DMA,
        ],
        compiler_params=pltpu.CompilerParams(vmem_limit_bytes=32 * 1024 * 1024),
        name="product",
    )(tile_live, row_panel, col_panel, keep)


def scale_body(x_ref, out_ref):
    parts, strips, height = x_ref.shape
    height = height - TILE
    nodes = parts * height
    unit = jnp.exp(x_ref[:, :, height:].astype(jnp.float32) * OCTAVE) * (1.0 / LEVELS)
    kept = [x_ref[:, :, at : at + TILE].astype(jnp.float32) * unit for at in range(0, height, TILE)]
    entries = jnp.concatenate([part * part for part in kept], axis=2)
    column_total = jnp.sum(jnp.sum(entries, axis=0), axis=1, keepdims=True)
    factor = nodes / column_total
    for p in range(parts):
        out_ref[0, :, p * height : (p + 1) * height] = entries[p] * factor


def scale(entries):
    parts, strips, height = entries.shape
    height = height - TILE
    return pl.pallas_call(
        scale_body,
        out_shape=jax.ShapeDtypeStruct((1, strips, parts * height), jnp.float32),
        in_specs=[pl.BlockSpec(memory_space=pltpu.VMEM)],
        out_specs=pl.BlockSpec(memory_space=pltpu.VMEM),
        compiler_params=pltpu.CompilerParams(vmem_limit_bytes=4 * 1024 * 1024),
        name="scale",
    )(entries)


def shards(transition, tile_live, prune_keep):
    packed = pack(tile_live, transition)
    col_panel = lax.all_gather(packed, "row", axis=0)
    packed, col_panel = lax.optimization_barrier((packed, col_panel))
    row_panel = lax.all_gather(packed, "col", axis=0)
    strips = product(tile_live, row_panel, col_panel, prune_keep)
    entries = lax.all_to_all(strips, "row", split_axis=0, concat_axis=0, tiled=True)
    return scale(entries)


def solution(mesh):
    placed = (P("row", "col"), P(), P("row", "col"))
    return jax.shard_map(
        shards, mesh=mesh, in_specs=placed, out_specs=P("col", "row", None), check_vma=False
    )
```

```python
import jax
import jax.numpy as jnp
from jax import lax
from jax.experimental import pallas as pl
from jax.experimental.pallas import tpu as pltpu
from jax.sharding import PartitionSpec as P

TILE = 128
LIVE = 4
UNIT = 16384.0
LEVELS = 32700.0
OCTAVE = 0.6931471805599453 / 1024
SMALLEST = 2.0**-20
PARTS = 2
GROUP = 8


def spots(rows, cols):
    return [(a, b, slice(a * TILE, (a + 1) * TILE), slice(b * TILE, (b + 1) * TILE)) for a in range(rows) for b in range(cols)]


def pack_body(live_hbm, x_hbm, out_ref, live, x_ref, arrived):
    rows, cols = x_ref.shape[0] // TILE, x_ref.shape[1] // TILE
    top, left = lax.axis_index("row") * rows, lax.axis_index("col") * cols
    group = pl.multiple_of(top // GROUP * GROUP, GROUP)
    flags_in = pltpu.make_async_copy(live_hbm.at[pl.ds(group, GROUP)], live, arrived.at[0])
    block_in = pltpu.make_async_copy(x_hbm, x_ref, arrived.at[1])
    flags_in.start()
    block_in.start()
    flags_in.wait()
    block_in.wait()
    top = top - group
    slot = jnp.int32(0)
    for a, b, across, down in spots(rows, cols):
        flag = live[top + a, left + b]

        @pl.when((flag > 0) & (slot < LIVE))
        def _(slot=slot, across=across, down=down):
            units = x_ref[across, down].astype(jnp.float32).T * UNIT
            out_ref[slot] = units.astype(jnp.int32).astype(jnp.int16)

        slot = slot + flag


def pack(tile_live, transition):
    return pl.pallas_call(
        pack_body,
        out_shape=jax.ShapeDtypeStruct((LIVE, TILE, TILE), jnp.int16),
        in_specs=[pl.BlockSpec(memory_space=pl.ANY)] * 2,
        out_specs=pl.BlockSpec(memory_space=pltpu.VMEM),
        scratch_shapes=[
            pltpu.SMEM((GROUP, tile_live.shape[1]), tile_live.dtype),
            pltpu.VMEM(transition.shape, transition.dtype),
            pltpu.SemaphoreType.DMA((2,)),
        ],
        name="pack",
    )(tile_live, transition)


def placing(live, top, left, rows, cols, slots_ref, dense_ref, down, across):
    slot, tasks = jnp.int32(0), []
    for spot, (a, b, _, _) in enumerate(spots(rows, cols)):
        flag = live[top + a, left + b]

        def place(flag=flag, slot=slot if spot < LIVE else jnp.minimum(slot, LIVE - 1), a=a, b=b):
            tile = slots_ref[slot].astype(jnp.float32)
            tile = jnp.where(flag > 0, tile, 0.0).astype(jnp.bfloat16)
            dense_ref[down + b * TILE : down + (b + 1) * TILE, across + a * TILE : across + (a + 1) * TILE] = tile

        tasks.append(place)
        slot = slot + flag
    return tasks


def product_body(rows, cols, live_hbm, a_ref, b_ref, keep_ref, out_ref, live, own, a_dense, b_dense, total, arrived):
    panels = a_ref.shape[0]
    each = b_ref.shape[0] // panels
    top, left = lax.axis_index("row") * rows, lax.axis_index("col") * cols
    group = pl.multiple_of(top // GROUP * GROUP, GROUP)
    behind = live.shape[0] - GROUP
    first = pltpu.make_async_copy(live_hbm.at[pl.ds(0, GROUP)], live.at[pl.ds(0, GROUP)], arrived.at[0])
    mine = pltpu.make_async_copy(live_hbm.at[pl.ds(group, GROUP)], own, arrived.at[1])
    rest = pltpu.make_async_copy(live_hbm.at[pl.ds(GROUP, behind)], live.at[pl.ds(GROUP, behind)], arrived.at[2])
    for flags in (first, mine, rest):
        flags.start()

    def tasks_of(panel):
        a_to, b_to = a_dense.at[panel % 2], b_dense.at[panel % 2]
        tasks = placing(own, top - group, panel * cols, rows, cols, a_ref.at[panel], a_to, 0, 0)
        for e in range(each):
            block = panel * each + e
            tasks += placing(live, block * rows, left, rows, cols, b_ref.at[block], b_to, 0, e * rows * TILE)
        return tasks

    keep = keep_ref[...].astype(jnp.float32).T * (1.0 / (UNIT * UNIT))
    first.wait()
    mine.wait()
    for place in tasks_of(0):
        place()
    for panel in range(panels):
        if panel + 1 == GROUP // (each * rows):
            rest.wait()
        later = tasks_of(panel + 1) if panel + 1 < panels else []
        share, high = len(later) // PARTS, total.shape[0] // PARTS
        for part in range(PARTS):
            lines = slice(part * high, (part + 1) * high)
            product = jnp.dot(
                b_dense[panel % 2, lines, :], a_dense[panel % 2], preferred_element_type=jnp.float32
            )
            total[lines, :] = product if panel == 0 else total[lines, :] + product
            for place in later[part * share : (part + 1) * share]:
                place()
    kept = total[...] * keep
    strips, height = out_ref.shape[:2], total.shape[1]
    largest = jnp.maximum(jnp.max(kept, axis=1, keepdims=True), SMALLEST)
    code = jnp.ceil(jnp.log(largest) * (1.0 / OCTAVE))
    levels = (kept * (LEVELS / jnp.exp(code * OCTAVE)) + 0.5).astype(jnp.int32).astype(jnp.int16)
    out_ref[:, :, :height] = levels.reshape(*strips, height)
    code = jnp.broadcast_to(code, (code.shape[0], TILE)).astype(jnp.int32).astype(jnp.int16)
    out_ref[:, :, height:] = code.reshape(*strips, TILE)


def product(tile_live, row_panel, col_panel, keep):
    n_row = col_panel.shape[0]
    height, width = keep.shape
    rows, cols = height // TILE, width // TILE
    in_vmem = pl.BlockSpec(memory_space=pltpu.VMEM)
    return pl.pallas_call(
        lambda *refs: product_body(rows, cols, *refs),
        out_shape=jax.ShapeDtypeStruct((n_row, width // n_row, height + TILE), jnp.int16),
        in_specs=[pl.BlockSpec(memory_space=pl.ANY), in_vmem, in_vmem, in_vmem],
        out_specs=in_vmem,
        scratch_shapes=[
            pltpu.SMEM(tile_live.shape, tile_live.dtype),
            pltpu.SMEM((GROUP, tile_live.shape[1]), tile_live.dtype),
            pltpu.VMEM((2, width, height), jnp.bfloat16),
            pltpu.VMEM((2, width, width), jnp.bfloat16),
            pltpu.VMEM((width, height), jnp.float32),
            pltpu.SemaphoreType.DMA((3,)),
        ],
        compiler_params=pltpu.CompilerParams(vmem_limit_bytes=32 * 1024 * 1024),
        name="product",
    )(tile_live, row_panel, col_panel, keep)


def scale_body(x_ref, out_ref):
    parts, strips, height = x_ref.shape
    height = height - TILE
    nodes = parts * height
    unit = jnp.exp(x_ref[:, :, height:].astype(jnp.float32) * OCTAVE) * (1.0 / LEVELS)
    kept = [x_ref[:, :, at : at + TILE].astype(jnp.float32) * unit for at in range(0, height, TILE)]
    entries = jnp.concatenate([part * part for part in kept], axis=2)
    column_total = jnp.sum(jnp.sum(entries, axis=0), axis=1, keepdims=True)
    factor = nodes / column_total
    for p in range(parts):
        out_ref[0, :, p * height : (p + 1) * height] = entries[p] * factor


def scale(entries):
    parts, strips, height = entries.shape
    height = height - TILE
    return pl.pallas_call(
        scale_body,
        out_shape=jax.ShapeDtypeStruct((1, strips, parts * height), jnp.float32),
        in_specs=[pl.BlockSpec(memory_space=pltpu.VMEM)],
        out_specs=pl.BlockSpec(memory_space=pltpu.VMEM),
        compiler_params=pltpu.CompilerParams(vmem_limit_bytes=4 * 1024 * 1024),
        name="scale",
    )(entries)


def shards(transition, tile_live, prune_keep):
    packed = pack(tile_live, transition)
    row_panel = lax.all_gather(packed, "col", axis=0)
    col_panel = lax.all_gather(packed, "row", axis=0)
    strips = product(tile_live, row_panel, col_panel, prune_keep)
    entries = lax.all_to_all(strips, "row", split_axis=0, concat_axis=0, tiled=True)
    return scale(entries)


def solution(mesh):
    placed = (P("row", "col"), P(), P("row", "col"))
    return jax.shard_map(
        shards, mesh=mesh, in_specs=placed, out_specs=P("col", "row", None), check_vma=False
    )
```

```python
import jax
import jax.numpy as jnp
from jax import lax
from jax.experimental import pallas as pl
from jax.experimental.pallas import tpu as pltpu
from jax.sharding import PartitionSpec as P

TILE = 128
LIVE = 4
UNIT = 16384.0
LEVELS = 32700.0
OCTAVE = 0.6931471805599453 / 1024
SMALLEST = 2.0**-20
PARTS = 2
GROUP = 8
CHUNKS = 4


def spots(rows, cols):
    return [(a, b, slice(a * TILE, (a + 1) * TILE), slice(b * TILE, (b + 1) * TILE)) for a in range(rows) for b in range(cols)]


def pack_body(live_hbm, x_hbm, out_ref, live, x_ref, arrived):
    rows, cols = x_ref.shape[0] // TILE, x_ref.shape[1] // TILE
    top, left = lax.axis_index("row") * rows, lax.axis_index("col") * cols
    group = pl.multiple_of(top // GROUP * GROUP, GROUP)
    flags_in = pltpu.make_async_copy(live_hbm.at[pl.ds(group, GROUP)], live, arrived.at[0])
    lines = [pl.ds(a * TILE, TILE) for a in range(rows)]
    block_in = [pltpu.make_async_copy(x_hbm.at[at], x_ref.at[at], arrived.at[1 + a]) for a, at in enumerate(lines)]
    flags_in.start()
    for line in block_in:
        line.start()
    flags_in.wait()
    top = top - group
    slot = jnp.int32(0)
    for a, b, across, down in spots(rows, cols):
        flag = live[top + a, left + b]
        if b == 0:
            block_in[a].wait()

        @pl.when((flag > 0) & (slot < LIVE))
        def _(slot=slot, across=across, down=down):
            units = x_ref[across, down].astype(jnp.float32).T * UNIT
            out_ref[slot] = units.astype(jnp.int32).astype(jnp.int16)

        slot = slot + flag


def pack(tile_live, transition):
    return pl.pallas_call(
        pack_body,
        out_shape=jax.ShapeDtypeStruct((LIVE, TILE, TILE), jnp.int16),
        in_specs=[pl.BlockSpec(memory_space=pl.ANY)] * 2,
        out_specs=pl.BlockSpec(memory_space=pltpu.VMEM),
        scratch_shapes=[
            pltpu.SMEM((GROUP, tile_live.shape[1]), tile_live.dtype),
            pltpu.VMEM(transition.shape, transition.dtype),
            pltpu.SemaphoreType.DMA((1 + transition.shape[0] // TILE,)),
        ],
        name="pack",
    )(tile_live, transition)


def placing(live, top, left, rows, cols, slots_ref, dense_ref, down, across):
    slot, tasks = jnp.int32(0), []
    for spot, (a, b, _, _) in enumerate(spots(rows, cols)):
        flag = live[top + a, left + b]

        def place(flag=flag, slot=slot if spot < LIVE else jnp.minimum(slot, LIVE - 1), a=a, b=b):
            tile = slots_ref[slot].astype(jnp.float32)
            tile = jnp.where(flag > 0, tile, 0.0).astype(jnp.bfloat16)
            dense_ref[down + b * TILE : down + (b + 1) * TILE, across + a * TILE : across + (a + 1) * TILE] = tile

        tasks.append(place)
        slot = slot + flag
    return tasks


def product_body(rows, cols, live_hbm, a_ref, b_ref, keep_ref, out_ref, live, own, a_dense, b_dense, total, arrived):
    panels = a_ref.shape[0]
    each = b_ref.shape[0] // panels
    top, left = lax.axis_index("row") * rows, lax.axis_index("col") * cols
    group = pl.multiple_of(top // GROUP * GROUP, GROUP)
    behind = live.shape[0] - GROUP
    first = pltpu.make_async_copy(live_hbm.at[pl.ds(0, GROUP)], live.at[pl.ds(0, GROUP)], arrived.at[0])
    mine = pltpu.make_async_copy(live_hbm.at[pl.ds(group, GROUP)], own, arrived.at[1])
    rest = pltpu.make_async_copy(live_hbm.at[pl.ds(GROUP, behind)], live.at[pl.ds(GROUP, behind)], arrived.at[2])
    for flags in (first, mine, rest):
        flags.start()

    def tasks_of(panel):
        a_to, b_to = a_dense.at[panel % 2], b_dense.at[panel % 2]
        tasks = placing(own, top - group, panel * cols, rows, cols, a_ref.at[panel], a_to, 0, 0)
        for e in range(each):
            block = panel * each + e
            tasks += placing(live, block * rows, left, rows, cols, b_ref.at[block], b_to, 0, e * rows * TILE)
        return tasks

    keep = keep_ref[...].astype(jnp.float32).T * (1.0 / (UNIT * UNIT))
    first.wait()
    mine.wait()
    for place in tasks_of(0):
        place()
    for panel in range(panels):
        if panel + 1 == GROUP // (each * rows):
            rest.wait()
        later = tasks_of(panel + 1) if panel + 1 < panels else []
        share, high = len(later) // PARTS, total.shape[0] // PARTS
        for part in range(PARTS):
            lines = slice(part * high, (part + 1) * high)
            product = jnp.dot(
                b_dense[panel % 2, lines, :], a_dense[panel % 2], preferred_element_type=jnp.float32
            )
            total[lines, :] = product if panel == 0 else total[lines, :] + product
            for place in later[part * share : (part + 1) * share]:
                place()
    kept = total[...] * keep
    strips, height = out_ref.shape[:2], total.shape[1]
    largest = jnp.maximum(jnp.max(kept, axis=1, keepdims=True), SMALLEST)
    code = jnp.ceil(jnp.log(largest) * (1.0 / OCTAVE))
    levels = (kept * (LEVELS / jnp.exp(code * OCTAVE)) + 0.5).astype(jnp.int32).astype(jnp.int16)
    out_ref[:, :, :height] = levels.reshape(*strips, height)
    code = jnp.broadcast_to(code, (code.shape[0], TILE)).astype(jnp.int32).astype(jnp.int16)
    out_ref[:, :, height:] = code.reshape(*strips, TILE)


def product(tile_live, row_panel, col_panel, keep):
    n_row = col_panel.shape[0]
    height, width = keep.shape
    rows, cols = height // TILE, width // TILE
    in_vmem = pl.BlockSpec(memory_space=pltpu.VMEM)
    return pl.pallas_call(
        lambda *refs: product_body(rows, cols, *refs),
        out_shape=jax.ShapeDtypeStruct((n_row, width // n_row, height + TILE), jnp.int16),
        in_specs=[pl.BlockSpec(memory_space=pl.ANY), in_vmem, in_vmem, in_vmem],
        out_specs=in_vmem,
        scratch_shapes=[
            pltpu.SMEM(tile_live.shape, tile_live.dtype),
            pltpu.SMEM((GROUP, tile_live.shape[1]), tile_live.dtype),
            pltpu.VMEM((2, width, height), jnp.bfloat16),
            pltpu.VMEM((2, width, width), jnp.bfloat16),
            pltpu.VMEM((width, height), jnp.float32),
            pltpu.SemaphoreType.DMA((3,)),
        ],
        compiler_params=pltpu.CompilerParams(vmem_limit_bytes=32 * 1024 * 1024),
        name="product",
    )(tile_live, row_panel, col_panel, keep)


def scale_body(x_ref, out_hbm, out_ref, sent):
    parts, strips, height = x_ref.shape
    height = height - TILE
    nodes = parts * height
    unit = jnp.exp(x_ref[:, :, height:].astype(jnp.float32) * OCTAVE) * (1.0 / LEVELS)
    kept = [x_ref[:, :, at : at + TILE].astype(jnp.float32) * unit for at in range(0, height, TILE)]
    entries = jnp.concatenate([part * part for part in kept], axis=2)
    column_total = jnp.sum(jnp.sum(entries, axis=0), axis=1, keepdims=True)
    factor = nodes / column_total
    copies = []
    for p in range(parts):
        out_ref[:, p * height : (p + 1) * height] = entries[p] * factor
        if (p + 1) % (parts // CHUNKS) == 0:
            chunk = p * CHUNKS // parts
            span = slice(chunk * nodes // CHUNKS, (chunk + 1) * nodes // CHUNKS)
            copies.append(pltpu.make_async_copy(out_ref.at[:, span], out_hbm.at[0, :, span], sent.at[chunk]))
            copies[-1].start()
    for copy in copies:
        copy.wait()


def scale(entries):
    parts, strips, height = entries.shape
    height = height - TILE
    return pl.pallas_call(
        scale_body,
        out_shape=jax.ShapeDtypeStruct((1, strips, parts * height), jnp.float32),
        in_specs=[pl.BlockSpec(memory_space=pltpu.VMEM)],
        out_specs=pl.BlockSpec(memory_space=pl.ANY),
        scratch_shapes=[pltpu.VMEM((strips, parts * height), jnp.float32), pltpu.SemaphoreType.DMA((CHUNKS,))],
        compiler_params=pltpu.CompilerParams(vmem_limit_bytes=4 * 1024 * 1024),
        name="scale",
    )(entries)


def shards(transition, tile_live, prune_keep):
    packed = pack(tile_live, transition)
    row_panel = lax.all_gather(packed, "col", axis=0)
    col_panel = lax.all_gather(packed, "row", axis=0)
    strips = product(tile_live, row_panel, col_panel, prune_keep)
    entries = lax.all_to_all(strips, "row", split_axis=0, concat_axis=0, tiled=True)
    return scale(entries)


def solution(mesh):
    placed = (P("row", "col"), P(), P("row", "col"))
    return jax.shard_map(
        shards, mesh=mesh, in_specs=placed, out_specs=P("col", "row", None), check_vma=False
    )
```

```python
import jax
import jax.numpy as jnp
from jax import lax
from jax.experimental import pallas as pl
from jax.experimental.pallas import tpu as pltpu
from jax.sharding import PartitionSpec as P

TILE = 128
LIVE = 4
UNIT = 16384.0
LEVELS = 32700.0
OCTAVE = 0.6931471805599453 / 1024
SMALLEST = 2.0**-20
PARTS = 2
PAIR = 2
GROUP = 8
CHUNKS = 4


def spots(rows, cols):
    return [(a, b, slice(a * TILE, (a + 1) * TILE), slice(b * TILE, (b + 1) * TILE)) for a in range(rows) for b in range(cols)]


def pack_body(live_hbm, x_hbm, out_ref, live, x_ref, arrived):
    rows, cols = x_ref.shape[0] // TILE, x_ref.shape[1] // TILE
    top, left = lax.axis_index("row") * rows, lax.axis_index("col") * cols
    group = pl.multiple_of(top // GROUP * GROUP, GROUP)
    flags_in = pltpu.make_async_copy(live_hbm.at[pl.ds(group, GROUP)], live, arrived.at[0])
    lines = [pl.ds(a * TILE, TILE) for a in range(rows)]
    block_in = [pltpu.make_async_copy(x_hbm.at[at], x_ref.at[at], arrived.at[1 + a]) for a, at in enumerate(lines)]
    flags_in.start()
    for line in block_in:
        line.start()
    flags_in.wait()
    top = top - group
    slot = jnp.int32(0)
    for a, b, across, down in spots(rows, cols):
        flag = live[top + a, left + b]
        if b == 0:
            block_in[a].wait()

        @pl.when((flag > 0) & (slot < LIVE))
        def _(slot=slot, across=across, down=down):
            units = x_ref[across, down].astype(jnp.float32).T * UNIT
            out_ref[slot] = units.astype(jnp.int32).astype(jnp.int16)

        slot = slot + flag


def pack(tile_live, transition):
    return pl.pallas_call(
        pack_body,
        out_shape=jax.ShapeDtypeStruct((LIVE, TILE, TILE), jnp.int16),
        in_specs=[pl.BlockSpec(memory_space=pl.ANY)] * 2,
        out_specs=pl.BlockSpec(memory_space=pltpu.VMEM),
        scratch_shapes=[
            pltpu.SMEM((GROUP, tile_live.shape[1]), tile_live.dtype),
            pltpu.VMEM(transition.shape, transition.dtype),
            pltpu.SemaphoreType.DMA((1 + transition.shape[0] // TILE,)),
        ],
        name="pack",
    )(tile_live, transition)


def placing(live, top, left, rows, cols, slots_ref, dense_ref, down, across):
    slot, tasks = jnp.int32(0), []
    for spot, (a, b, _, _) in enumerate(spots(rows, cols)):
        flag = live[top + a, left + b]

        def place(flag=flag, slot=slot if spot < LIVE else jnp.minimum(slot, LIVE - 1), a=a, b=b):
            tile = slots_ref[slot].astype(jnp.float32)
            tile = jnp.where(flag > 0, tile, 0.0).astype(jnp.bfloat16)
            dense_ref[down + b * TILE : down + (b + 1) * TILE, across + a * TILE : across + (a + 1) * TILE] = tile

        tasks.append(place)
        slot = slot + flag
    return tasks


def product_body(rows, cols, live_hbm, a_ref, b_ref, keep_ref, out_ref, live, own, a_dense, b_dense, total, arrived):
    panels = a_ref.shape[0]
    each = b_ref.shape[0] // panels
    top, left = lax.axis_index("row") * rows, lax.axis_index("col") * cols
    group = pl.multiple_of(top // GROUP * GROUP, GROUP)
    behind = live.shape[0] - GROUP
    first = pltpu.make_async_copy(live_hbm.at[pl.ds(0, GROUP)], live.at[pl.ds(0, GROUP)], arrived.at[0])
    mine = pltpu.make_async_copy(live_hbm.at[pl.ds(group, GROUP)], own, arrived.at[1])
    rest = pltpu.make_async_copy(live_hbm.at[pl.ds(GROUP, behind)], live.at[pl.ds(GROUP, behind)], arrived.at[2])
    for flags in (first, mine, rest):
        flags.start()

    def tasks_of(pair):
        a_to, b_to = a_dense.at[pair % 2], b_dense.at[pair % 2]
        tasks = []
        for p in range(PAIR):
            panel = pair * PAIR + p
            tasks += placing(own, top - group, panel * cols, rows, cols, a_ref.at[panel], a_to, p * cols * TILE, 0)
            for e in range(each):
                block = panel * each + e
                across = (p * each + e) * rows * TILE
                tasks += placing(live, block * rows, left, rows, cols, b_ref.at[block], b_to, 0, across)
        return tasks

    keep = keep_ref[...].astype(jnp.float32).T * (1.0 / (UNIT * UNIT))
    first.wait()
    mine.wait()
    for place in tasks_of(0):
        place()
    for panel in range(panels // PAIR):
        if (panel + 1) * PAIR == GROUP // (each * rows):
            rest.wait()
        later = tasks_of(panel + 1) if (panel + 1) * PAIR < panels else []
        share, high = len(later) // PARTS, total.shape[0] // PARTS
        for part in range(PARTS):
            lines = slice(part * high, (part + 1) * high)
            product = jnp.dot(
                b_dense[panel % 2, lines, :], a_dense[panel % 2], preferred_element_type=jnp.float32
            )
            total[lines, :] = product if panel == 0 else total[lines, :] + product
            for place in later[part * share : (part + 1) * share]:
                place()
    kept = total[...] * keep
    strips, height = out_ref.shape[:2], total.shape[1]
    largest = jnp.maximum(jnp.max(kept, axis=1, keepdims=True), SMALLEST)
    code = jnp.ceil(jnp.log(largest) * (1.0 / OCTAVE))
    levels = (kept * (LEVELS / jnp.exp(code * OCTAVE)) + 0.5).astype(jnp.int32).astype(jnp.int16)
    out_ref[:, :, :height] = levels.reshape(*strips, height)
    code = jnp.broadcast_to(code, (code.shape[0], TILE)).astype(jnp.int32).astype(jnp.int16)
    out_ref[:, :, height:] = code.reshape(*strips, TILE)


def product(tile_live, row_panel, col_panel, keep):
    n_row = col_panel.shape[0]
    height, width = keep.shape
    rows, cols = height // TILE, width // TILE
    in_vmem = pl.BlockSpec(memory_space=pltpu.VMEM)
    return pl.pallas_call(
        lambda *refs: product_body(rows, cols, *refs),
        out_shape=jax.ShapeDtypeStruct((n_row, width // n_row, height + TILE), jnp.int16),
        in_specs=[pl.BlockSpec(memory_space=pl.ANY), in_vmem, in_vmem, in_vmem],
        out_specs=in_vmem,
        scratch_shapes=[
            pltpu.SMEM(tile_live.shape, tile_live.dtype),
            pltpu.SMEM((GROUP, tile_live.shape[1]), tile_live.dtype),
            pltpu.VMEM((2, PAIR * width, height), jnp.bfloat16),
            pltpu.VMEM((2, width, PAIR * width), jnp.bfloat16),
            pltpu.VMEM((width, height), jnp.float32),
            pltpu.SemaphoreType.DMA((3,)),
        ],
        compiler_params=pltpu.CompilerParams(vmem_limit_bytes=32 * 1024 * 1024),
        name="product",
    )(tile_live, row_panel, col_panel, keep)


def scale_body(x_ref, out_hbm, out_ref, sent):
    parts, strips, height = x_ref.shape
    height = height - TILE
    nodes = parts * height
    unit = jnp.exp(x_ref[:, :, height:].astype(jnp.float32) * OCTAVE) * (1.0 / LEVELS)
    kept = [x_ref[:, :, at : at + TILE].astype(jnp.float32) * unit for at in range(0, height, TILE)]
    entries = jnp.concatenate([part * part for part in kept], axis=2)
    column_total = jnp.sum(jnp.sum(entries, axis=0), axis=1, keepdims=True)
    factor = nodes / column_total
    copies = []
    for p in range(parts):
        out_ref[:, p * height : (p + 1) * height] = entries[p] * factor
        if (p + 1) % (parts // CHUNKS) == 0:
            chunk = p * CHUNKS // parts
            span = slice(chunk * nodes // CHUNKS, (chunk + 1) * nodes // CHUNKS)
            copies.append(pltpu.make_async_copy(out_ref.at[:, span], out_hbm.at[0, :, span], sent.at[chunk]))
            copies[-1].start()
    for copy in copies:
        copy.wait()


def scale(entries):
    parts, strips, height = entries.shape
    height = height - TILE
    return pl.pallas_call(
        scale_body,
        out_shape=jax.ShapeDtypeStruct((1, strips, parts * height), jnp.float32),
        in_specs=[pl.BlockSpec(memory_space=pltpu.VMEM)],
        out_specs=pl.BlockSpec(memory_space=pl.ANY),
        scratch_shapes=[pltpu.VMEM((strips, parts * height), jnp.float32), pltpu.SemaphoreType.DMA((CHUNKS,))],
        compiler_params=pltpu.CompilerParams(vmem_limit_bytes=4 * 1024 * 1024),
        name="scale",
    )(entries)


def shards(transition, tile_live, prune_keep):
    packed = pack(tile_live, transition)
    row_panel = lax.all_gather(packed, "col", axis=0)
    col_panel = lax.all_gather(packed, "row", axis=0)
    strips = product(tile_live, row_panel, col_panel, prune_keep)
    entries = lax.all_to_all(strips, "row", split_axis=0, concat_axis=0, tiled=True)
    return scale(entries)


def solution(mesh):
    placed = (P("row", "col"), P(), P("row", "col"))
    return jax.shard_map(
        shards, mesh=mesh, in_specs=placed, out_specs=P("col", "row", None), check_vma=False
    )
```
